32 devices in a mesh: groups: 2 (over y), img: 4 (over z), filt: 2 (over x), chan: 2 (over core).
Axes of the slice: x: 2, y: 2, z: 4, core: 2. Of those that a mesh axis runs over, the one named last changes fastest.
Arguments:
- images: float32 [16, 3, 32, 128], P(('groups', 'img', 'chan')), parts along dimension 0, may hold values from -24 to 24
- coefficients: bfloat16 [16, 256, 32, 128], P(('groups', 'img', 'chan'), 'filt'), parts along dimension 0, may hold values from -1.5 to 1.5
- dictionary: float32 [256, 363], P(('filt', 'img')), may hold values from -0.3 to 0.3
Outputs:
- coefficients_out: bfloat16 [16, 256, 32, 128], P(('groups', 'img', 'chan'), 'filt'), parts along dimension 0
- dictionary_out: float32 [512, 363], P(('groups', 'filt', 'img')), parts along dimension 0
The draws below stay inside these ranges and needn't reach their ends.
There are 2 independent parts, one for each index of `groups`. The reference program is written for one: setup_inputs(seed, part) draws one part's arguments, and reference() takes and returns one part's arrays. A program takes and returns all parts, laid end to end along the dimension named above; an argument that names none is the same for every part. Nothing has to cross between parts.
All inputs are finite; a program needn't handle non-finite values.
Results may differ from the reference program's by a relative error of at most 0.018.
Values may be sent and summed in bfloat16 or wider, within the bound.
A program may use at most 128 MiB of HBM per device.

```python
import math
import jax
import jax.numpy as jnp
from jax import lax

K = 256
TAPS = 363
ITERS = 2
HEIGHT = 32
WIDTH = 128
IMGS = 8


def draw_images(key, part):
    key = jax.random.fold_in(key, 11)
    first = jax.random.fold_in(key, 0)
    shape = (IMGS, 3, HEIGHT, WIDTH)
    scale = 2.0 * (1.0 + 2.0 * jnp.arange(IMGS, dtype=jnp.float32) / max(IMGS - 1, 1))
    base = jax.random.truncated_normal(first, -4.0, 4.0, shape, jnp.float32)
    return jnp.clip(base * scale[:, None, None, None], -24.0, 24.0)


def draw_coefficients(key, part):
    key = jax.random.fold_in(key, 23)
    first = jax.random.fold_in(key, 0)
    shape = (IMGS, K, HEIGHT, WIDTH)
    factor = 0.25 * (0.5 + jnp.arange(K, dtype=jnp.float32) / K)
    base = jax.random.truncated_normal(first, -4.0, 4.0, shape, jnp.float32)
    values = base * factor[None, :, None, None]
    return jnp.clip(values, -1.5, 1.5).astype(jnp.bfloat16)


def draw_dictionary(key, part):
    key = jax.random.fold_in(key, 37)
    first, second = jax.random.split(key)
    lengths = jnp.exp(jax.random.uniform(second, (K, 1), jnp.float32, math.log(0.7), math.log(1.4)))
    base = jax.random.truncated_normal(first, -4.0, 4.0, (K, TAPS), jnp.float32)
    return jnp.clip(base * lengths / math.sqrt(TAPS), -0.3, 0.3)


def setup_inputs(seed: int = 0, part: int = 0) -> dict:
    seeds = jax.random.split(jax.random.key(seed), 4)
    part_keys = jax.random.split(jax.random.fold_in(seeds[3], part), 4)
    return {
        "images": draw_images(jax.random.fold_in(jax.random.fold_in(seeds[3], part), 71), part),
        "coefficients": draw_coefficients(jax.random.fold_in(jax.random.fold_in(seeds[3], part), 71), part),
        "dictionary": draw_dictionary(jax.random.fold_in(seeds[3], 71), part),
    }


CODE_STEP = 0.04
SHRINK = 0.15
FILTER_STEP = 0.02
EPSILON = 1e-06

def shrink_values(values):
    return jnp.sign(values) * jnp.maximum(jnp.abs(values) - SHRINK, 0.0)

def patch_matrix(resid_image):
    padded = jnp.pad(resid_image, ((0, 0), (5, 5), (5, 5)))
    pieces = [padded[:, tap_row:tap_row + HEIGHT, tap_col:tap_col + WIDTH] for tap_row in range(11) for tap_col in range(11)]
    return jnp.stack(pieces, axis=1).reshape(TAPS, HEIGHT * WIDTH)

def reference(images, coefficients, dictionary):
    filters = dictionary
    current = coefficients
    for iteration in range(ITERS):
        filters_bf = filters.astype(jnp.bfloat16)
        kernel = filters_bf.astype(jnp.float32).reshape(K, 3, 11, 11)
        flipped = jnp.transpose(kernel, (1, 0, 2, 3))[:, :, ::-1, ::-1]
        flat_kernel = kernel.reshape(K, TAPS)

        def one_image(carry, pair):
            coeff_image, image = pair
            coeff_float = coeff_image.astype(jnp.float32)
            recon = lax.conv_general_dilated(coeff_float[None], flipped, (1, 1), ((5, 5), (5, 5)), precision=lax.Precision.HIGHEST)[0]
            resid = (recon - image).astype(jnp.bfloat16)
            columns = patch_matrix(resid.astype(jnp.float32))
            flat = coeff_float.reshape(K, HEIGHT * WIDTH)
            code_grad = jnp.dot(flat_kernel, columns, precision=lax.Precision.HIGHEST)
            updated = shrink_values(flat - CODE_STEP * code_grad).astype(jnp.bfloat16)
            carry = carry + jnp.dot(flat, columns.T, precision=lax.Precision.HIGHEST)
            return (carry, updated.reshape(K, HEIGHT, WIDTH))
        filter_grad, current = lax.scan(one_image, jnp.zeros((K, TAPS), jnp.float32), (current, images))
        grad_scale = jnp.sqrt(jnp.mean(filter_grad * filter_grad) + EPSILON)
        moved = filters - FILTER_STEP * filter_grad / grad_scale
        lengths = jnp.sqrt(lax.optimization_barrier(jnp.sum(moved * moved, axis=1, keepdims=True)))
        filters = moved / jnp.maximum(lengths, 1.0)
    return (current, filters)
```

```python
import functools
import jax
import jax.numpy as jnp
import numpy as np
from jax import lax
from jax.experimental import pallas as pl
from jax.experimental.pallas import tpu as pltpu
from jax.sharding import PartitionSpec as P

ITERS = 2
SIDE = 11
HALF = SIDE // 2
COLORS = 3
CODE_STEP = 0.04
SHRINK = 0.15
FILTER_STEP = 0.02
EPSILON = 1e-06

BLOCK = 40
ROWS = 448
GROUP = 8
SPAN = GROUP + SIDE - 1
LANES = 128
MESH = pl.DeviceIdType.MESH
F32 = jnp.float32
BF16 = jnp.bfloat16


def tap_order(taps, width):
    order = np.zeros((width, ROWS), np.float32)
    for tap in range(taps):
        color, rest = divmod(tap, SIDE * SIDE)
        row, col = divmod(rest, SIDE)
        order[tap, col * BLOCK + row * COLORS + color] = 1.0
    return order.astype(jnp.bfloat16)


def roll_columns(values, shift):
    if shift == 0:
        return values
    column = lax.broadcasted_iota(jnp.int32, values.shape, 1)
    rolled = pltpu.roll(values, shift % LANES, 1)
    inside = (column >= shift) & (column < LANES + shift)
    return jnp.where(inside, rolled, 0.0)


def kernel(
    sizes, count,
    img_ref, coef_hbm, dict_ref, order_ref,
    cout_ref, dout_ref,
    cpad, patches, toep, dtp, xb, image_rows,
    fil_bf, fil32, rec, gtx, grx, gall, glast, sqs,
    local_sem, send_sem, recv_sem,
):
    n_img, n_filt, n_chan = sizes
    n = n_img * n_chan
    n_part = n * n_filt
    height, width = img_ref.shape[1], img_ref.shape[2]
    pixels = height * width
    rows = height * COLORS
    kp = cpad.shape[0]
    share = fil32.shape[1]
    piece = share // n_chan
    taps = dict_ref.shape[1]
    groups = height // GROUP
    gr = GROUP * COLORS

    img, filt, chan = (lax.axis_index(a) for a in ("img", "filt", "chan"))
    me = img * n_chan + chan
    me_part = me * n_filt + filt

    def img_peers():
        return [{"img": lax.rem(img + s, n_img)} for s in range(1, n_img)]

    def filt_peers():
        return [{"filt": lax.rem(filt + s, n_filt)} for s in range(1, n_filt)]

    def chan_peers():
        return [{"chan": lax.rem(chan + s, n_chan)} for s in range(1, n_chan)]

    def set_peers():
        peers = []
        for s in range(1, n):
            other = lax.rem(me + s, n)
            peers.append((other, {"img": other // n_chan, "chan": lax.rem(other, n_chan)}))
        return peers

    def part_loop(body):
        def step(s, carry):
            other = lax.rem(me_part + s, n_part)
            place = other // n_filt
            body({
                "img": place // n_chan,
                "chan": lax.rem(place, n_chan),
                "filt": lax.rem(other, n_filt),
            })
            return carry
        lax.fori_loop(1, n_part, step, 0)

    def push(src, dst, sem, device):
        pltpu.make_async_remote_copy(
            src_ref=src, dst_ref=dst, send_sem=send_sem.at[sem], recv_sem=recv_sem.at[sem],
            device_id=device, device_id_type=MESH,
        ).start()

    def wait_in(view, sem):
        pltpu.make_async_copy(view, view, recv_sem.at[sem]).wait()

    def wait_out(view, sem):
        pltpu.make_async_copy(view, view, send_sem.at[sem]).wait()

    load = pltpu.make_async_copy(
        coef_hbm, cpad.at[:, pl.ds(HALF * width, pixels)], local_sem
    )
    load.start()

    barrier = pltpu.get_barrier_semaphore()
    part_loop(lambda d: pl.semaphore_signal(barrier, inc=1, device_id=d, device_id_type=MESH))

    own = jnp.zeros((share, fil32.shape[2]), F32)
    fil32[img] = own
    fil32[img, :, :taps] = dict_ref[...]
    fil_bf[img] = fil32[img].astype(BF16)

    edge = HALF * width
    cpad[:, :edge] = jnp.zeros((kp, edge), BF16)
    cpad[:, edge + pixels:] = jnp.zeros((kp, cpad.shape[1] - edge - pixels), BF16)
    dtp[...] = jnp.zeros(dtp.shape, F32)
    xb[...] = jnp.zeros(xb.shape, F32)
    for color in range(COLORS):
        image_rows[pl.ds(color, height, stride=COLORS), :] = img_ref[color]

    pl.semaphore_wait(barrier, n_part - 1)
    for d in img_peers():
        push(fil_bf.at[img], fil_bf.at[img], 0, d)
    for d in img_peers():
        push(fil32.at[img], fil32.at[img], 1, d)
    if n_img > 1:
        wait_in(fil_bf.at[pl.ds(0, n_img - 1)], 0)

    filters = fil_bf[...].reshape(kp, fil_bf.shape[2])
    for it in range(ITERS):
        last = it == ITERS - 1
        base = 2 + it * 4
        ordered = jnp.dot(filters, order_ref[...], preferred_element_type=F32)
        flipped = ordered.T
        for col in range(SIDE):
            dtp[col, gr:gr + BLOCK, :] = flipped[col * BLOCK:(col + 1) * BLOCK]
        for row in range(SPAN):
            start = gr + COLORS * (SIDE - 1 - row)
            parts = [dtp[col, start:start + gr, :] for col in range(SIDE)]
            spare = toep.shape[0] - SIDE * gr
            parts.append(jnp.zeros((spare, kp), F32))
            toep[:, row * kp:(row + 1) * kp] = jnp.concatenate(parts, 0).astype(BF16)
        if it == 0:
            load.wait()
        shifted = jnp.concatenate([
            jnp.concatenate([
                cpad[:, (g * GROUP + row) * width:(g * GROUP + row + 1) * width]
                for g in range(groups)
            ], 1) for row in range(SPAN)
        ], 0)
        summed = jnp.dot(toep[...], shifted, preferred_element_type=F32)
        share_sum = None
        for col in range(SIDE):
            block = jnp.concatenate([
                summed[col * gr:(col + 1) * gr, g * width:(g + 1) * width] for g in range(groups)
            ], 0)
            term = roll_columns(block, col - HALF)
            share_sum = term if share_sum is None else share_sum + term
        rec[it, filt] = share_sum
        for d in filt_peers():
            push(rec.at[it, filt], rec.at[it, filt], base, d)
        if n_filt > 1:
            wait_in(rec.at[it, pl.ds(0, n_filt - 1)], base)
        recon = rec[it, 0]
        for f in range(1, n_filt):
            recon = recon + rec[it, f]
        resid = (recon - image_rows[...]).astype(BF16).astype(F32)

        for col in range(SIDE):
            xb[col, 16:16 + rows, :] = roll_columns(resid, HALF - col)
        for y in range(height):
            start = COLORS * y + 1
            parts = [xb[col, start:start + BLOCK, :] for col in range(SIDE)]
            parts.append(jnp.zeros((ROWS - SIDE * BLOCK, width), F32))
            patches[:, y * width:(y + 1) * width] = jnp.concatenate(parts, 0).astype(BF16)

        grad = lax.dot_general(
            cpad[:, edge:edge + pixels], patches[...], (((1,), (1,)), ((), ())),
            preferred_element_type=F32,
        )
        plain = lax.dot_general(
            grad.astype(BF16), order_ref[...], (((1,), (1,)), ((), ())),
            preferred_element_type=F32,
        ).astype(BF16)
        gtx[it] = plain.reshape(n, piece, plain.shape[1])
        grx[it, me] = gtx[it, me]
        for other, d in set_peers():
            push(gtx.at[it, other], grx.at[it, me], base + 1, d)

        ordered_bf = ordered.astype(BF16)
        step = 4 * width
        for start in range(0, pixels, step):
            moved = cpad[:, edge + start:edge + start + step].astype(F32) - CODE_STEP * jnp.dot(
                ordered_bf, patches[:, start:start + step], preferred_element_type=F32
            )
            fresh = (moved - jnp.clip(moved, -SHRINK, SHRINK)).astype(BF16)
            if last:
                cout_ref[:, start:start + step] = fresh
            else:
                cpad[:, edge + start:edge + start + step] = fresh

        if n > 1:
            wait_in(grx.at[it, pl.ds(0, n - 1)], base + 1)
        total = grx[it, 0].astype(F32)
        for s in range(1, n):
            total = total + grx[it, s].astype(F32)
        total_bf = total.astype(BF16)
        total = total_bf.astype(F32)
        square = jnp.sum(jnp.sum(total * total, axis=1, keepdims=True), axis=0, keepdims=True)
        sqs[it, me_part] = jnp.broadcast_to(square, sqs.shape[2:])
        part_loop(lambda d: push(sqs.at[it, me_part], sqs.at[it, me_part], base + 3, d))
        if last:
            glast[chan] = total_bf
            for d in chan_peers():
                push(glast.at[chan], glast.at[chan], base + 2, d)
            if n_chan > 1:
                wait_in(glast.at[pl.ds(0, n_chan - 1)], base + 2)
            gradient = glast[...].reshape(share, glast.shape[2]).astype(F32)
            current = fil32[img]
        else:
            gall[it, me] = total_bf
            for other, d in set_peers():
                push(gall.at[it, me], gall.at[it, me], base + 2, d)
            if it == 0 and n_img > 1:
                wait_in(fil32.at[pl.ds(0, n_img - 1)], 1)
                wait_out(fil32.at[pl.ds(0, n_img - 1)], 1)
            if n > 1:
                wait_in(gall.at[it, pl.ds(0, n - 1)], base + 2)
            gradient = gall[it].reshape(kp, gall.shape[3]).astype(F32)
            current = fil32[...].reshape(kp, fil32.shape[2])
        if n_part > 1:
            wait_in(sqs.at[it, pl.ds(0, n_part - 1)], base + 3)
        squares = jnp.sum(sqs[it], axis=0)[:1, :1]
        scale = jnp.sqrt(squares / count + EPSILON)
        moved = current - FILTER_STEP * gradient / scale
        lengths = jnp.sqrt(jnp.sum(moved * moved, axis=1, keepdims=True))
        moved = moved / jnp.maximum(lengths, 1.0)
        if last:
            dout_ref[...] = moved[:, :taps]
        else:
            fil32[...] = moved.reshape(fil32.shape)
            filters = moved.astype(BF16)

    if n_img > 1:
        wait_out(fil_bf.at[pl.ds(0, n_img - 1)], 0)
    for it in range(ITERS):
        base = 2 + it * 4
        if n_filt > 1:
            wait_out(rec.at[it, pl.ds(0, n_filt - 1)], base)
        if n > 1:
            wait_out(grx.at[it, pl.ds(0, n - 1)], base + 1)
        if it == ITERS - 1:
            if n_chan > 1:
                wait_out(glast.at[pl.ds(0, n_chan - 1)], base + 2)
        elif n > 1:
            wait_out(gall.at[it, pl.ds(0, n - 1)], base + 2)
        if n_part > 1:
            wait_out(sqs.at[it, pl.ds(0, n_part - 1)], base + 3)


def per_device(sizes, images, coefficients, dictionary):
    n_img, n_filt, n_chan = sizes
    n = n_img * n_chan
    _, filters, height, width = coefficients.shape
    held, taps = dictionary.shape
    pixels = height * width
    share = -(-held // (16 * n_chan)) * 16 * n_chan
    kp = share * n_img
    lanes = -(-taps // LANES) * LANES
    coef = coefficients.reshape(n_img, held, pixels)
    coef = jnp.pad(coef, ((0, 0), (0, share - held), (0, 0))).reshape(kp, pixels)
    dictionary = jnp.pad(dictionary, ((0, share - held), (0, 0)))
    order = jnp.asarray(tap_order(taps, lanes))
    gr = GROUP * COLORS
    toep_rows = -(-SIDE * gr // 16) * 16
    dtp_rows = gr + COLORS * (SIDE - 1) + gr + 2
    sems = 2 + 4 * ITERS
    vmem = pl.BlockSpec(memory_space=pltpu.VMEM)
    out_coef, out_dict = pl.pallas_call(
        functools.partial(kernel, sizes, float(filters * n_filt * taps)),
        out_shape=(
            jax.ShapeDtypeStruct((kp, pixels), BF16),
            jax.ShapeDtypeStruct((share, taps), F32),
        ),
        in_specs=[vmem, pl.BlockSpec(memory_space=pl.ANY), vmem, vmem],
        out_specs=(vmem, vmem),
        scratch_shapes=[
            pltpu.VMEM((kp, (height + 2 * HALF) * width), BF16),
            pltpu.VMEM((ROWS, pixels), BF16),
            pltpu.VMEM((toep_rows, SPAN * kp), BF16),
            pltpu.VMEM((SIDE, dtp_rows, kp), F32),
            pltpu.VMEM((SIDE, COLORS * (height - 1) + BLOCK + 3, width), F32),
            pltpu.VMEM((COLORS * height, width), F32),
            pltpu.VMEM((n_img, share, lanes), BF16),
            pltpu.VMEM((n_img, share, lanes), F32),
            pltpu.VMEM((ITERS, n_filt, COLORS * height, width), F32),
            pltpu.VMEM((ITERS, n, share // n_chan, lanes), BF16),
            pltpu.VMEM((ITERS, n, share // n_chan, lanes), BF16),
            pltpu.VMEM((ITERS - 1, n, share // n_chan, lanes), BF16),
            pltpu.VMEM((n_chan, share // n_chan, lanes), BF16),
            pltpu.VMEM((ITERS, n * n_filt, 8, LANES), F32),
            pltpu.SemaphoreType.DMA,
            pltpu.SemaphoreType.DMA((sems,)),
            pltpu.SemaphoreType.DMA((sems,)),
        ],
        compiler_params=pltpu.CompilerParams(
            collective_id=0, has_side_effects=True, vmem_limit_bytes=56 * 2**20
        ),
        name="dictionary_steps",
    )(images[0], coef, dictionary, order)
    out_coef = out_coef.reshape(n_img, share, height, width)[:, :held]
    return out_coef.reshape(1, filters, height, width), out_dict[:held]


def solution(mesh):
    sizes = tuple(mesh.shape[a] for a in ("img", "filt", "chan"))
    placed = (
        P(("groups", "img", "chan"), None, None, None),
        P(("groups", "img", "chan"), "filt", None, None),
        P(("filt", "img"), None),
    )
    return jax.shard_map(
        functools.partial(per_device, sizes),
        mesh=mesh,
        in_specs=placed,
        out_specs=(
            P(("groups", "img", "chan"), "filt", None, None),
            P(("groups", "filt", "img"), None),
        ),
        check_vma=False,
    )
```

```python
import functools
import jax
import jax.numpy as jnp
import numpy as np
from jax import lax
from jax.experimental import pallas as pl
from jax.experimental.pallas import tpu as pltpu
from jax.sharding import PartitionSpec as P

ITERS = 2
SIDE = 11
HALF = SIDE // 2
COLORS = 3
CODE_STEP = 0.04
SHRINK = 0.15
FILTER_STEP = 0.02
EPSILON = 1e-06

BLOCK = 40
ROWS = 448
GROUP = 8
SPAN = GROUP + SIDE - 1
LANES = 128
MESH = pl.DeviceIdType.MESH
F32 = jnp.float32
BF16 = jnp.bfloat16


def tap_order(taps, width):
    order = np.zeros((width, ROWS), np.float32)
    for tap in range(taps):
        color, rest = divmod(tap, SIDE * SIDE)
        row, col = divmod(rest, SIDE)
        order[tap, col * BLOCK + row * COLORS + color] = 1.0
    return order.astype(jnp.bfloat16)


def roll_columns(values, shift):
    if shift == 0:
        return values
    column = lax.broadcasted_iota(jnp.int32, values.shape, 1)
    rolled = pltpu.roll(values, shift % LANES, 1)
    inside = (column >= shift) & (column < LANES + shift)
    return jnp.where(inside, rolled, 0.0)


def kernel(
    sizes, count,
    img_ref, coef_hbm, dict_ref, order_hbm,
    cout_hbm, dout_ref,
    native, cpad, patches, toep, dtp, xb, image_rows, order_ref, fresh_rows, cout_bf,
    fil_bf, fil32, rec, gtx, grx, gall, glast, sqs,
    local_sem, send_sem, recv_sem,
):
    n_img, n_filt, n_chan = sizes
    n = n_img * n_chan
    n_part = n * n_filt
    height, width = img_ref.shape[1], img_ref.shape[2]
    pixels = height * width
    rows = height * COLORS
    kp = cpad.shape[0]
    share = fil32.shape[1]
    piece = share // n_chan
    taps = dict_ref.shape[1]
    groups = height // GROUP
    gr = GROUP * COLORS

    img, filt, chan = (lax.axis_index(a) for a in ("img", "filt", "chan"))
    me = img * n_chan + chan
    me_part = me * n_filt + filt

    def img_peers():
        return [{"img": lax.rem(img + s, n_img)} for s in range(1, n_img)]

    def filt_peers():
        return [{"filt": lax.rem(filt + s, n_filt)} for s in range(1, n_filt)]

    def chan_peers():
        return [{"chan": lax.rem(chan + s, n_chan)} for s in range(1, n_chan)]

    def set_peers():
        peers = []
        for s in range(1, n):
            other = lax.rem(me + s, n)
            peers.append((other, {"img": other // n_chan, "chan": lax.rem(other, n_chan)}))
        return peers

    def part_loop(body):
        def step(s, carry):
            other = me_part + s
            other = jnp.where(other >= n_part, other - n_part, other)
            place = other // n_filt
            body({
                "img": place // n_chan,
                "chan": lax.rem(place, n_chan),
                "filt": lax.rem(other, n_filt),
            })
            return carry
        if n_part > 32:
            lax.fori_loop(1, n_part, step, 0)
        else:
            for s in range(1, n_part):
                step(s, 0)

    def push(src, dst, sem, device):
        pltpu.make_async_remote_copy(
            src_ref=src, dst_ref=dst, send_sem=send_sem.at[sem], recv_sem=recv_sem.at[sem],
            device_id=device, device_id_type=MESH,
        ).start()

    def wait_in(view, sem):
        pltpu.make_async_copy(view, view, recv_sem.at[sem]).wait()

    def wait_out(view, sem):
        pltpu.make_async_copy(view, view, send_sem.at[sem]).wait()

    barrier = pltpu.get_barrier_semaphore()
    load = pltpu.make_async_copy(coef_hbm, native, local_sem.at[0])
    load.start()
    load_order = pltpu.make_async_copy(order_hbm, order_ref, local_sem.at[1])
    load_order.start()
    part_loop(lambda d: pl.semaphore_signal(barrier, inc=1, device_id=d, device_id_type=MESH))

    own = jnp.zeros((share, fil32.shape[2]), F32)
    fil32[img] = own
    fil32[img, :, :taps] = dict_ref[...]
    fil_bf[img] = fil32[img].astype(BF16)

    edge = HALF * width
    cpad[:, :edge] = jnp.zeros((kp, edge), BF16)
    cpad[:, edge + pixels:] = jnp.zeros((kp, cpad.shape[1] - edge - pixels), BF16)
    dtp[...] = jnp.zeros(dtp.shape, F32)
    xb[...] = jnp.zeros(xb.shape, F32)
    for color in range(COLORS):
        image_rows[pl.ds(color, height, stride=COLORS), :] = img_ref[color]

    pl.semaphore_wait(barrier, n_part - 1)
    for d in img_peers():
        push(fil_bf.at[img], fil_bf.at[img], 0, d)
    load.wait()
    for y in range(0, height, 16):
        fresh_rows[...] = native[:, y:y + 16, :].astype(F32)
        for r in range(16):
            at = edge + (y + r) * width
            cpad[:, at:at + width] = fresh_rows[:, r, :].astype(BF16)
    load_order.wait()
    if n_img > 1:
        wait_in(fil_bf.at[pl.ds(0, n_img - 1)], 0)

    filters = fil_bf[...].reshape(kp, fil_bf.shape[2])
    for it in range(ITERS):
        last = it == ITERS - 1
        base = 2 + it * 4
        ordered = jnp.dot(filters, order_ref[...], preferred_element_type=F32)
        flipped = ordered.T
        for col in range(SIDE):
            dtp[col, gr:gr + BLOCK, :] = flipped[col * BLOCK:(col + 1) * BLOCK]
        for row in range(SPAN):
            start = gr + COLORS * (SIDE - 1 - row)
            parts = [dtp[col, start:start + gr, :] for col in range(SIDE)]
            spare = toep.shape[0] - SIDE * gr
            parts.append(jnp.zeros((spare, kp), F32))
            toep[:, row * kp:(row + 1) * kp] = jnp.concatenate(parts, 0).astype(BF16)
        shifted = jnp.concatenate([
            jnp.concatenate([
                cpad[:, (g * GROUP + row) * width:(g * GROUP + row + 1) * width]
                for g in range(groups)
            ], 1) for row in range(SPAN)
        ], 0)
        summed = jnp.dot(toep[...], shifted, preferred_element_type=F32)
        share_sum = None
        for col in range(SIDE):
            block = jnp.concatenate([
                summed[col * gr:(col + 1) * gr, g * width:(g + 1) * width] for g in range(groups)
            ], 0)
            term = roll_columns(block, col - HALF)
            share_sum = term if share_sum is None else share_sum + term
        rec[it, filt] = share_sum
        for d in filt_peers():
            push(rec.at[it, filt], rec.at[it, filt], base, d)
        if it == 0:
            for d in img_peers():
                push(fil32.at[img], fil32.at[img], 1, d)
        if n_filt > 1:
            wait_in(rec.at[it, pl.ds(0, n_filt - 1)], base)
        recon = rec[it, 0]
        for f in range(1, n_filt):
            recon = recon + rec[it, f]
        resid = (recon - image_rows[...]).astype(BF16).astype(F32)

        for col in range(SIDE):
            xb[col, 16:16 + rows, :] = roll_columns(resid, HALF - col)
        for y in range(height):
            start = COLORS * y + 1
            parts = [xb[col, start:start + BLOCK, :] for col in range(SIDE)]
            parts.append(jnp.zeros((ROWS - SIDE * BLOCK, width), F32))
            patches[:, y * width:(y + 1) * width] = jnp.concatenate(parts, 0).astype(BF16)

        grad = lax.dot_general(
            cpad[:, edge:edge + pixels], patches[...], (((1,), (1,)), ((), ())),
            preferred_element_type=F32,
        )
        plain = lax.dot_general(
            grad.astype(BF16), order_ref[...], (((1,), (1,)), ((), ())),
            preferred_element_type=F32,
        ).astype(BF16)
        gtx[it] = plain.reshape(n, piece, plain.shape[1])
        grx[it, me] = gtx[it, me]
        for other, d in set_peers():
            push(gtx.at[it, other], grx.at[it, me], base + 1, d)

        ordered_bf = ordered.astype(BF16)
        step = 4 * width
        for start in range(0, pixels, step):
            moved = cpad[:, edge + start:edge + start + step].astype(F32) - CODE_STEP * jnp.dot(
                ordered_bf, patches[:, start:start + step], preferred_element_type=F32
            )
            fresh = (moved - jnp.clip(moved, -SHRINK, SHRINK)).astype(BF16)
            if last:
                y = start // width
                for r in range(4):
                    fresh_rows[:, y % 16 + r, :] = fresh[:, r * width:(r + 1) * width].astype(F32)
                if (y + 4) % 16 == 0:
                    cout_bf[:, y - 12:y + 4, :] = fresh_rows[...].astype(BF16)
            else:
                cpad[:, edge + start:edge + start + step] = fresh

        if last:
            store = pltpu.make_async_copy(cout_bf, cout_hbm, local_sem.at[0])
            store.start()
        if n > 1:
            wait_in(grx.at[it, pl.ds(0, n - 1)], base + 1)
        total = grx[it, 0].astype(F32)
        for s in range(1, n):
            total = total + grx[it, s].astype(F32)
        total_bf = total.astype(BF16)
        total = total_bf.astype(F32)
        square = jnp.sum(jnp.sum(total * total, axis=1, keepdims=True), axis=0, keepdims=True)
        sqs[it, me_part] = jnp.broadcast_to(square, sqs.shape[2:])
        part_loop(lambda d: push(sqs.at[it, me_part], sqs.at[it, me_part], base + 3, d))
        if last:
            glast[chan] = total_bf
            for d in chan_peers():
                push(glast.at[chan], glast.at[chan], base + 2, d)
            if n_chan > 1:
                wait_in(glast.at[pl.ds(0, n_chan - 1)], base + 2)
            gradient = glast[...].reshape(share, glast.shape[2]).astype(F32)
            current = fil32[img]
        else:
            gall[it, me] = total_bf
            for other, d in set_peers():
                push(gall.at[it, me], gall.at[it, me], base + 2, d)
            if it == 0 and n_img > 1:
                wait_in(fil32.at[pl.ds(0, n_img - 1)], 1)
                wait_out(fil32.at[pl.ds(0, n_img - 1)], 1)
            if n > 1:
                wait_in(gall.at[it, pl.ds(0, n - 1)], base + 2)
            gradient = gall[it].reshape(kp, gall.shape[3]).astype(F32)
            current = fil32[...].reshape(kp, fil32.shape[2])
        if n_part > 1:
            wait_in(sqs.at[it, pl.ds(0, n_part - 1)], base + 3)
        squares = jnp.sum(sqs[it], axis=0)[:, :1]
        scale = jnp.sqrt(squares / count + EPSILON)
        moved = current - FILTER_STEP * gradient / scale
        lengths = jnp.sqrt(jnp.sum(moved * moved, axis=1, keepdims=True))
        moved = moved / jnp.maximum(lengths, 1.0)
        if last:
            dout_ref[...] = moved[:, :taps]
        else:
            fil32[...] = moved.reshape(fil32.shape)
            filters = moved.astype(BF16)

    store.wait()
    if n_img > 1:
        wait_out(fil_bf.at[pl.ds(0, n_img - 1)], 0)
    for it in range(ITERS):
        base = 2 + it * 4
        if n_filt > 1:
            wait_out(rec.at[it, pl.ds(0, n_filt - 1)], base)
        if n > 1:
            wait_out(grx.at[it, pl.ds(0, n - 1)], base + 1)
        if it == ITERS - 1:
            if n_chan > 1:
                wait_out(glast.at[pl.ds(0, n_chan - 1)], base + 2)
        elif n > 1:
            wait_out(gall.at[it, pl.ds(0, n - 1)], base + 2)
        if n_part > 1:
            wait_out(sqs.at[it, pl.ds(0, n_part - 1)], base + 3)


def per_device(sizes, images, coefficients, dictionary):
    n_img, n_filt, n_chan = sizes
    n = n_img * n_chan
    _, filters, height, width = coefficients.shape
    held, taps = dictionary.shape
    pixels = height * width
    share = -(-held // (16 * n_chan)) * 16 * n_chan
    kp = share * n_img
    lanes = -(-taps // LANES) * LANES
    coef = coefficients.reshape(n_img, held, height, width)
    coef = jnp.pad(coef, ((0, 0), (0, share - held), (0, 0), (0, 0)))
    coef = coef.reshape(kp, height, width)
    dictionary = jnp.pad(dictionary, ((0, share - held), (0, 0)))
    order = jnp.asarray(tap_order(taps, lanes))
    gr = GROUP * COLORS
    toep_rows = -(-SIDE * gr // 16) * 16
    dtp_rows = gr + COLORS * (SIDE - 1) + gr + 2
    sems = 2 + 4 * ITERS
    vmem = pl.BlockSpec(memory_space=pltpu.VMEM)
    hbm = pl.BlockSpec(memory_space=pl.ANY)
    out_coef, out_dict = pl.pallas_call(
        functools.partial(kernel, sizes, float(filters * n_filt * taps)),
        out_shape=(
            jax.ShapeDtypeStruct((kp, height, width), BF16),
            jax.ShapeDtypeStruct((share, taps), F32),
        ),
        in_specs=[vmem, hbm, vmem, hbm],
        out_specs=(hbm, vmem),
        scratch_shapes=[
            pltpu.VMEM((kp, height, width), BF16),
            pltpu.VMEM((kp, (height + 2 * HALF) * width), BF16),
            pltpu.VMEM((ROWS, pixels), BF16),
            pltpu.VMEM((toep_rows, SPAN * kp), BF16),
            pltpu.VMEM((SIDE, dtp_rows, kp), F32),
            pltpu.VMEM((SIDE, COLORS * (height - 1) + BLOCK + 3, width), F32),
            pltpu.VMEM((COLORS * height, width), F32),
            pltpu.VMEM((lanes, ROWS), BF16),
            pltpu.VMEM((kp, 16, width), F32),
            pltpu.VMEM((kp, height, width), BF16),
            pltpu.VMEM((n_img, share, lanes), BF16),
            pltpu.VMEM((n_img, share, lanes), F32),
            pltpu.VMEM((ITERS, n_filt, COLORS * height, width), F32),
            pltpu.VMEM((ITERS, n, share // n_chan, lanes), BF16),
            pltpu.VMEM((ITERS, n, share // n_chan, lanes), BF16),
            pltpu.VMEM((ITERS - 1, n, share // n_chan, lanes), BF16),
            pltpu.VMEM((n_chan, share // n_chan, lanes), BF16),
            pltpu.VMEM((ITERS, n * n_filt, 1, LANES), F32),
            pltpu.SemaphoreType.DMA((2,)),
            pltpu.SemaphoreType.DMA((sems,)),
            pltpu.SemaphoreType.DMA((sems,)),
        ],
        compiler_params=pltpu.CompilerParams(
            collective_id=0, has_side_effects=True, vmem_limit_bytes=56 * 2**20
        ),
        name="dictionary_steps",
    )(images[0], coef, dictionary, order)
    out_coef = out_coef.reshape(n_img, share, height, width)[:, :held]
    return out_coef.reshape(1, filters, height, width), out_dict[:held]


def solution(mesh):
    sizes = tuple(mesh.shape[a] for a in ("img", "filt", "chan"))
    placed = (
        P(("groups", "img", "chan"), None, None, None),
        P(("groups", "img", "chan"), "filt", None, None),
        P(("filt", "img"), None),
    )
    return jax.shard_map(
        functools.partial(per_device, sizes),
        mesh=mesh,
        in_specs=placed,
        out_specs=(
            P(("groups", "img", "chan"), "filt", None, None),
            P(("groups", "filt", "img"), None),
        ),
        check_vma=False,
    )
```

```python
import functools
import jax
import jax.numpy as jnp
import numpy as np
from jax import lax
from jax.experimental import pallas as pl
from jax.experimental.pallas import tpu as pltpu
from jax.sharding import PartitionSpec as P

ITERS = 2
SIDE = 11
HALF = SIDE // 2
COLORS = 3
CODE_STEP = 0.04
SHRINK = 0.15
FILTER_STEP = 0.02
EPSILON = 1e-06

BLOCK = 40
ROWS = 448
GROUP = 8
SPAN = GROUP + SIDE - 1
LANES = 128
MESH = pl.DeviceIdType.MESH
F32 = jnp.float32
BF16 = jnp.bfloat16


def tap_order(taps, width):
    order = np.zeros((width, ROWS), np.float32)
    for tap in range(taps):
        color, rest = divmod(tap, SIDE * SIDE)
        row, col = divmod(rest, SIDE)
        order[tap, col * BLOCK + row * COLORS + color] = 1.0
    return order.astype(jnp.bfloat16)


def roll_columns(values, shift):
    if shift == 0:
        return values
    column = lax.broadcasted_iota(jnp.int32, values.shape, 1)
    rolled = pltpu.roll(values, shift % LANES, 1)
    inside = (column >= shift) & (column < LANES + shift)
    return jnp.where(inside, rolled, 0.0)


def kernel(
    sizes, count,
    img_ref, coef_hbm, dict_ref, order_hbm,
    cout_hbm, dout_ref,
    native, cpad, patches, toep, dtp, xb, image_rows, order_ref, fresh_rows, cout_bf,
    fil_bf, fil32, rec, gtx, grx, gall, glast, sqs,
    local_sem, send_sem, recv_sem,
):
    n_img, n_filt, n_chan = sizes
    n = n_img * n_chan
    n_part = n * n_filt
    height, width = img_ref.shape[1], img_ref.shape[2]
    pixels = height * width
    rows = height * COLORS
    kp = cpad.shape[0]
    share = fil32.shape[1]
    piece = share // n_chan
    taps = dict_ref.shape[1]
    groups = height // GROUP
    gr = GROUP * COLORS

    img, filt, chan = (lax.axis_index(a) for a in ("img", "filt", "chan"))
    me = img * n_chan + chan
    me_part = me * n_filt + filt

    def img_peers():
        return [{"img": lax.rem(img + s, n_img)} for s in range(1, n_img)]

    def filt_peers():
        return [{"filt": lax.rem(filt + s, n_filt)} for s in range(1, n_filt)]

    def chan_peers():
        return [{"chan": lax.rem(chan + s, n_chan)} for s in range(1, n_chan)]

    def set_peers():
        peers = []
        for s in range(1, n):
            other = lax.rem(me + s, n)
            peers.append((other, {"img": other // n_chan, "chan": lax.rem(other, n_chan)}))
        return peers

    def part_loop(body):
        def step(s, carry):
            other = me_part + s
            other = jnp.where(other >= n_part, other - n_part, other)
            place = other // n_filt
            body({
                "img": place // n_chan,
                "chan": lax.rem(place, n_chan),
                "filt": lax.rem(other, n_filt),
            })
            return carry
        if n_part > 32:
            lax.fori_loop(1, n_part, step, 0)
        else:
            for s in range(1, n_part):
                step(s, 0)

    def push(src, dst, sem, device):
        pltpu.make_async_remote_copy(
            src_ref=src, dst_ref=dst, send_sem=send_sem.at[sem], recv_sem=recv_sem.at[sem],
            device_id=device, device_id_type=MESH,
        ).start()

    def wait_in(view, sem):
        pltpu.make_async_copy(view, view, recv_sem.at[sem]).wait()

    def wait_out(view, sem):
        pltpu.make_async_copy(view, view, send_sem.at[sem]).wait()

    barrier = pltpu.get_barrier_semaphore()
    load = pltpu.make_async_copy(coef_hbm, native, local_sem.at[0])
    load.start()
    load_order = pltpu.make_async_copy(order_hbm, order_ref, local_sem.at[1])
    load_order.start()
    part_loop(lambda d: pl.semaphore_signal(barrier, inc=1, device_id=d, device_id_type=MESH))

    own = jnp.zeros((share, fil32.shape[2]), F32)
    fil32[img] = own
    fil32[img, :, :taps] = dict_ref[...]
    fil_bf[img] = fil32[img].astype(BF16)

    edge = HALF * width
    cpad[:, :edge] = jnp.zeros((kp, edge), BF16)
    cpad[:, edge + pixels:] = jnp.zeros((kp, cpad.shape[1] - edge - pixels), BF16)
    dtp[...] = jnp.zeros(dtp.shape, F32)
    xb[...] = jnp.zeros(xb.shape, F32)
    for color in range(COLORS):
        image_rows[pl.ds(color, height, stride=COLORS), :] = img_ref[color]

    pl.semaphore_wait(barrier, n_part - 1)
    for d in img_peers():
        push(fil_bf.at[img], fil_bf.at[img], 0, d)
    load.wait()
    for y in range(0, height, 16):
        fresh_rows[...] = native[:, y:y + 16, :].astype(F32)
        for r in range(16):
            at = edge + (y + r) * width
            cpad[:, at:at + width] = fresh_rows[:, r, :].astype(BF16)
    load_order.wait()
    if n_img > 1:
        wait_in(fil_bf.at[pl.ds(0, n_img - 1)], 0)

    filters = fil_bf[...].reshape(kp, fil_bf.shape[2])
    for it in range(ITERS):
        last = it == ITERS - 1
        base = 2 + it * 4
        ordered = jnp.dot(filters, order_ref[...], preferred_element_type=F32)
        flipped = ordered.T
        for col in range(SIDE):
            dtp[col, gr:gr + BLOCK, :] = flipped[col * BLOCK:(col + 1) * BLOCK]
        for row in range(SPAN):
            start = gr + COLORS * (SIDE - 1 - row)
            parts = [dtp[col, start:start + gr, :] for col in range(SIDE)]
            spare = toep.shape[0] - SIDE * gr
            parts.append(jnp.zeros((spare, kp), F32))
            toep[:, row * kp:(row + 1) * kp] = jnp.concatenate(parts, 0).astype(BF16)
        shifted = jnp.concatenate([
            jnp.concatenate([
                cpad[:, (g * GROUP + row) * width:(g * GROUP + row + 1) * width]
                for g in range(groups)
            ], 1) for row in range(SPAN)
        ], 0)
        summed = jnp.dot(toep[...], shifted, preferred_element_type=F32)
        share_sum = None
        for col in range(SIDE):
            block = jnp.concatenate([
                summed[col * gr:(col + 1) * gr, g * width:(g + 1) * width] for g in range(groups)
            ], 0)
            term = roll_columns(block, col - HALF)
            share_sum = term if share_sum is None else share_sum + term
        rec[it, filt] = share_sum.astype(BF16)
        for d in filt_peers():
            push(rec.at[it, filt], rec.at[it, filt], base, d)
        if it == 0:
            for d in img_peers():
                push(fil32.at[img], fil32.at[img], 1, d)
        if n_filt > 1:
            wait_in(rec.at[it, pl.ds(0, n_filt - 1)], base)
        recon = share_sum
        for s in range(1, n_filt):
            recon = recon + rec[it, lax.rem(filt + s, n_filt)].astype(F32)
        resid = (recon - image_rows[...]).astype(BF16).astype(F32)

        for col in range(SIDE):
            xb[col, 16:16 + rows, :] = roll_columns(resid, HALF - col)
        for y in range(height):
            start = COLORS * y + 1
            parts = [xb[col, start:start + BLOCK, :] for col in range(SIDE)]
            parts.append(jnp.zeros((ROWS - SIDE * BLOCK, width), F32))
            patches[:, y * width:(y + 1) * width] = jnp.concatenate(parts, 0).astype(BF16)

        grad = lax.dot_general(
            cpad[:, edge:edge + pixels], patches[...], (((1,), (1,)), ((), ())),
            preferred_element_type=F32,
        )
        plain = lax.dot_general(
            grad.astype(BF16), order_ref[...], (((1,), (1,)), ((), ())),
            preferred_element_type=F32,
        ).astype(BF16)
        gtx[it] = plain.reshape(n, piece, plain.shape[1])
        grx[it, me] = gtx[it, me]
        for other, d in set_peers():
            push(gtx.at[it, other], grx.at[it, me], base + 1, d)

        ordered_bf = ordered.astype(BF16)
        step = 4 * width
        for start in range(0, pixels, step):
            moved = cpad[:, edge + start:edge + start + step].astype(F32) - CODE_STEP * jnp.dot(
                ordered_bf, patches[:, start:start + step], preferred_element_type=F32
            )
            fresh = (moved - jnp.clip(moved, -SHRINK, SHRINK)).astype(BF16)
            if last:
                y = start // width
                for r in range(4):
                    fresh_rows[:, y % 16 + r, :] = fresh[:, r * width:(r + 1) * width].astype(F32)
                if (y + 4) % 16 == 0:
                    cout_bf[:, y - 12:y + 4, :] = fresh_rows[...].astype(BF16)
            else:
                cpad[:, edge + start:edge + start + step] = fresh

        if last:
            store = pltpu.make_async_copy(cout_bf, cout_hbm, local_sem.at[0])
            store.start()
        if n > 1:
            wait_in(grx.at[it, pl.ds(0, n - 1)], base + 1)
        total = grx[it, 0].astype(F32)
        for s in range(1, n):
            total = total + grx[it, s].astype(F32)
        total_bf = total.astype(BF16)
        total = total_bf.astype(F32)
        square = jnp.sum(jnp.sum(total * total, axis=1, keepdims=True), axis=0, keepdims=True)
        sqs[it, me_part] = jnp.broadcast_to(square, sqs.shape[2:])
        if last:
            part_loop(lambda d: push(sqs.at[it, me_part], sqs.at[it, me_part], base + 3, d))
            glast[chan] = total_bf
            for d in chan_peers():
                push(glast.at[chan], glast.at[chan], base + 2, d)
            if n_chan > 1:
                wait_in(glast.at[pl.ds(0, n_chan - 1)], base + 2)
            gradient = glast[...].reshape(share, glast.shape[2]).astype(F32)
            current = fil32[img]
        else:
            gall[it, me] = total_bf
            for other, d in set_peers():
                push(gall.at[it, me], gall.at[it, me], base + 2, d)
            part_loop(lambda d: push(sqs.at[it, me_part], sqs.at[it, me_part], base + 3, d))
            if it == 0 and n_img > 1:
                wait_in(fil32.at[pl.ds(0, n_img - 1)], 1)
                wait_out(fil32.at[pl.ds(0, n_img - 1)], 1)
            if n > 1:
                wait_in(gall.at[it, pl.ds(0, n - 1)], base + 2)
            gradient = gall[it].reshape(kp, gall.shape[3]).astype(F32)
            current = fil32[...].reshape(kp, fil32.shape[2])
        if n_part > 1:
            wait_in(sqs.at[it, pl.ds(0, n_part - 1)], base + 3)
        squares = jnp.sum(sqs[it], axis=0)[:, :1]
        scale = jnp.sqrt(squares / count + EPSILON)
        moved = current - FILTER_STEP * gradient / scale
        lengths = jnp.sqrt(jnp.sum(moved * moved, axis=1, keepdims=True))
        moved = moved / jnp.maximum(lengths, 1.0)
        if last:
            dout_ref[...] = moved[:, :taps]
        else:
            fil32[...] = moved.reshape(fil32.shape)
            filters = moved.astype(BF16)

    store.wait()
    if n_img > 1:
        wait_out(fil_bf.at[pl.ds(0, n_img - 1)], 0)
    for it in range(ITERS):
        base = 2 + it * 4
        if n_filt > 1:
            wait_out(rec.at[it, pl.ds(0, n_filt - 1)], base)
        if n > 1:
            wait_out(grx.at[it, pl.ds(0, n - 1)], base + 1)
        if it == ITERS - 1:
            if n_chan > 1:
                wait_out(glast.at[pl.ds(0, n_chan - 1)], base + 2)
        elif n > 1:
            wait_out(gall.at[it, pl.ds(0, n - 1)], base + 2)
        if n_part > 1:
            wait_out(sqs.at[it, pl.ds(0, n_part - 1)], base + 3)


def per_device(sizes, images, coefficients, dictionary):
    n_img, n_filt, n_chan = sizes
    n = n_img * n_chan
    _, filters, height, width = coefficients.shape
    held, taps = dictionary.shape
    pixels = height * width
    share = -(-held // (16 * n_chan)) * 16 * n_chan
    kp = share * n_img
    lanes = -(-taps // LANES) * LANES
    coef = coefficients.reshape(n_img, held, height, width)
    coef = jnp.pad(coef, ((0, 0), (0, share - held), (0, 0), (0, 0)))
    coef = coef.reshape(kp, height, width)
    dictionary = jnp.pad(dictionary, ((0, share - held), (0, 0)))
    order = jnp.asarray(tap_order(taps, lanes))
    gr = GROUP * COLORS
    toep_rows = -(-SIDE * gr // 16) * 16
    dtp_rows = gr + COLORS * (SIDE - 1) + gr + 2
    sems = 2 + 4 * ITERS
    vmem = pl.BlockSpec(memory_space=pltpu.VMEM)
    hbm = pl.BlockSpec(memory_space=pl.ANY)
    out_coef, out_dict = pl.pallas_call(
        functools.partial(kernel, sizes, float(filters * n_filt * taps)),
        out_shape=(
            jax.ShapeDtypeStruct((kp, height, width), BF16),
            jax.ShapeDtypeStruct((share, taps), F32),
        ),
        in_specs=[vmem, hbm, vmem, hbm],
        out_specs=(hbm, vmem),
        scratch_shapes=[
            pltpu.VMEM((kp, height, width), BF16),
            pltpu.VMEM((kp, (height + 2 * HALF) * width), BF16),
            pltpu.VMEM((ROWS, pixels), BF16),
            pltpu.VMEM((toep_rows, SPAN * kp), BF16),
            pltpu.VMEM((SIDE, dtp_rows, kp), F32),
            pltpu.VMEM((SIDE, COLORS * (height - 1) + BLOCK + 3, width), F32),
            pltpu.VMEM((COLORS * height, width), F32),
            pltpu.VMEM((lanes, ROWS), BF16),
            pltpu.VMEM((kp, 16, width), F32),
            pltpu.VMEM((kp, height, width), BF16),
            pltpu.VMEM((n_img, share, lanes), BF16),
            pltpu.VMEM((n_img, share, lanes), F32),
            pltpu.VMEM((ITERS, n_filt, COLORS * height, width), BF16),
            pltpu.VMEM((ITERS, n, share // n_chan, lanes), BF16),
            pltpu.VMEM((ITERS, n, share // n_chan, lanes), BF16),
            pltpu.VMEM((ITERS - 1, n, share // n_chan, lanes), BF16),
            pltpu.VMEM((n_chan, share // n_chan, lanes), BF16),
            pltpu.VMEM((ITERS, n * n_filt, 1, LANES), F32),
            pltpu.SemaphoreType.DMA((2,)),
            pltpu.SemaphoreType.DMA((sems,)),
            pltpu.SemaphoreType.DMA((sems,)),
        ],
        compiler_params=pltpu.CompilerParams(
            collective_id=0, has_side_effects=True, vmem_limit_bytes=56 * 2**20
        ),
        name="dictionary_steps",
    )(images[0], coef, dictionary, order)
    out_coef = out_coef.reshape(n_img, share, height, width)[:, :held]
    return out_coef.reshape(1, filters, height, width), out_dict[:held]


def solution(mesh):
    sizes = tuple(mesh.shape[a] for a in ("img", "filt", "chan"))
    placed = (
        P(("groups", "img", "chan"), None, None, None),
        P(("groups", "img", "chan"), "filt", None, None),
        P(("filt", "img"), None),
    )
    return jax.shard_map(
        functools.partial(per_device, sizes),
        mesh=mesh,
        in_specs=placed,
        out_specs=(
            P(("groups", "img", "chan"), "filt", None, None),
            P(("groups", "filt", "img"), None),
        ),
        check_vma=False,
    )
```
